32 devices in a mesh: parts: 2 (over y), band: 4 (over z), win: 2 (over x), rep: 2 (over core).
Axes of the slice: x: 2, y: 2, z: 4, core: 2. Of those that a mesh axis runs over, the one named last changes fastest.
Arguments:
- records: bfloat16 [8, 15360, 512], P(('parts', 'win'), 'rep', 'band'), parts along dimension 0, may hold values from -30 to 30
- bin_first: int32 [1], replicated, may hold values from 56 to 66
- pair_blocks: int32 [4, 4, 2], P('band'), may hold values from 0 to 3, as said below
- pair_counts: int32 [4], P('band'), may hold values from 1 to 4
Outputs:
- cross: float32 [1088, 4, 128, 256], P(('parts', 'band'), 'rep', 'win'), parts along dimension 0
The draws below stay inside these ranges and needn't reach their ends.
There are 2 independent parts, one for each index of `parts`. The reference program is written for one: setup_inputs(seed, part) draws one part's arguments, and reference() takes and returns one part's arrays. A program takes and returns all parts, laid end to end along the dimension named above; an argument that names none is the same for every part. Nothing has to cross between parts.
Inputs may be any that keep to these rules, and one draw needn't show every extreme that they name: `pair_blocks`: row s of band b names blocks i <= j of the 4 channel blocks with j - i <= 8.
All inputs are finite; a program needn't handle non-finite values.
Results may differ from the reference program's by a relative error of at most 0.015.
Values may be sent and summed in bfloat16 or wider, within the bound.
A program may use at most 128 MiB of HBM per device.

```python
import math
import jax
import jax.numpy as jnp
from jax import lax

PAIR_SLOTS = 4
SAMPLES = 15360
NBINS = 544
BLOCK = 128
MAXOFF = 8
GROUPS = 2
BANDS = 4
WINDOWS = 4
CHANNELS = 512


def draw_records(key, part):
    key = jax.random.fold_in(key, 11)
    key_noise, key_chan, key_win = jax.random.split(key, 3)
    chan_gain = jnp.exp(jax.random.uniform(key_chan, (1, 1, CHANNELS), jnp.float32, math.log(0.3), math.log(3.0)))
    win_gain = jnp.exp(jax.random.uniform(key_win, (WINDOWS, 1, 1), jnp.float32, math.log(0.5), math.log(2.0)))
    base = jnp.clip(jax.random.normal(key_noise, (WINDOWS, SAMPLES, CHANNELS), jnp.float32), -5.0, 5.0)
    return (base * chan_gain * win_gain).astype(jnp.bfloat16)


def draw_pair_blocks(key, part):
    key = jax.random.fold_in(key, 23)
    key_first, key_offset = jax.random.split(key, 2)
    blocks = CHANNELS // BLOCK
    first = jax.random.randint(key_first, (BANDS, PAIR_SLOTS), 0, blocks, jnp.int32)
    offset = jax.random.randint(key_offset, (BANDS, PAIR_SLOTS), 0, MAXOFF + 1, jnp.int32)
    first = first.at[0, 0].set(blocks - 1)
    first = first.at[0, 1].set(0)
    second = jnp.minimum(first + offset, blocks - 1)
    return jnp.stack([first, second], axis=-1).astype(jnp.int32)


def draw_pair_counts(key, part):
    key = jax.random.fold_in(key, 37)
    band = jnp.arange(BANDS, dtype=jnp.int32)
    lower = jax.random.randint(key, (BANDS,), 0, 2, jnp.int32) * (band > 0).astype(jnp.int32)
    counts = PAIR_SLOTS - band * PAIR_SLOTS // BANDS - lower
    return jnp.maximum(counts, 1).astype(jnp.int32)


def setup_inputs(seed: int = 0, part: int = 0) -> dict:
    key_of = jax.random.split(jax.random.key(seed), 5)
    part_keys = jax.random.split(jax.random.fold_in(key_of[4], part), 5)
    return {
        "records": draw_records(jax.random.fold_in(jax.random.fold_in(key_of[4], part), 71), part),
        "bin_first": jax.random.randint(key_of[1], (1,), 56, 67).astype(jnp.int32),
        "pair_blocks": draw_pair_blocks(jax.random.fold_in(key_of[4], 71), part),
        "pair_counts": draw_pair_counts(jax.random.fold_in(key_of[4], 71), part),
    }


water_level = 0.1

def dft_basis(start, rows, first, nbins, samples):
    times = start + lax.iota(jnp.int32, rows)
    freqs = first + lax.iota(jnp.int32, nbins)
    phase_index = times[:, None] * freqs[None, :] % samples
    phase = phase_index.astype(jnp.float32) * (2.0 * math.pi / samples)
    return jnp.concatenate([jnp.cos(phase), -jnp.sin(phase)], axis=1).astype(jnp.bfloat16)

def whiten(spectrum):
    count, doubled, width = spectrum.shape
    nbins = doubled // 2
    split = spectrum.reshape(count, 2, nbins, width)
    power = split[:, 0] * split[:, 0] + split[:, 1] * split[:, 1]
    level = jnp.sqrt(lax.optimization_barrier(jnp.mean(power, axis=1)) + 1e-06)
    denom = jnp.sqrt(power) + water_level * level[:, None, :]
    return split / denom[:, None]

def cross_terms(left, right, groups, total):
    count = left.shape[0]
    per_group = count // groups
    nbins = left.shape[2]
    left32 = left.astype(jnp.float32)
    right32 = right.astype(jnp.float32)
    rotated = jnp.stack([jnp.concatenate([right32[:, 0], -right32[:, 1]], axis=-1), jnp.concatenate([right32[:, 1], right32[:, 0]], axis=-1)], axis=1)
    left_groups = left32.reshape(groups, per_group, 2, nbins, left.shape[3])
    right_groups = rotated.reshape(groups, per_group, 2, nbins, rotated.shape[3])
    return jnp.einsum('gwpfr,gwpfc->gfrc', left_groups, right_groups, precision=lax.Precision.HIGHEST) / total

def reference(records, bin_first, pair_blocks, pair_counts):
    windows, samples, channels = records.shape
    rows = 1280 if samples % 1280 == 0 else samples
    first = bin_first[0]

    def step(carry, index):
        begin = index * rows
        basis = dft_basis(begin, rows, first, NBINS, SAMPLES)
        piece = lax.dynamic_slice_in_dim(records, begin, rows, 1)
        update = jnp.einsum('wtc,tk->wkc', piece.astype(jnp.float32), basis.astype(jnp.float32), precision=lax.Precision.HIGHEST)
        return (carry + update, None)
    start = jnp.zeros((windows, 2 * NBINS, channels), jnp.float32)
    spectrum, _ = lax.scan(step, start, jnp.arange(samples // rows, dtype=jnp.int32))
    white = whiten(spectrum).astype(jnp.bfloat16)
    band_bins = NBINS // BANDS

    def band_cross(band):
        band_spec = lax.dynamic_slice_in_dim(white, band * band_bins, band_bins, 2)
        pairs = pair_blocks[band]
        live_count = pair_counts[band]
        results = []
        for slot in range(PAIR_SLOTS):
            left = lax.dynamic_slice_in_dim(band_spec, pairs[slot, 0] * BLOCK, BLOCK, 3)
            right = lax.dynamic_slice_in_dim(band_spec, pairs[slot, 1] * BLOCK, BLOCK, 3)
            term = cross_terms(left, right, GROUPS, windows)
            rounded = lax.optimization_barrier(term.astype(jnp.bfloat16))
            summed = lax.optimization_barrier(jnp.sum(rounded.astype(jnp.float32), axis=0))
            live = (slot < live_count).astype(jnp.float32)
            results.append(summed * live)
        return jnp.stack(results, axis=1)
    crosses = lax.map(band_cross, jnp.arange(BANDS, dtype=jnp.int32))
    return crosses.reshape(NBINS, PAIR_SLOTS, BLOCK, 2 * BLOCK)
```

```python
import functools
import math

import jax
import jax.numpy as jnp
from jax import lax
from jax.experimental import pallas as pl
from jax.experimental.pallas import tpu as pltpu
from jax.sharding import PartitionSpec as P

SAMPLES = 15360
NBINS = 544
BLOCK = 128
LANES = 128
SUB = 8
ROWS = 1280
MESH = pl.DeviceIdType.MESH

water_level = 0.1


def rotor(times, freqs):
    turns = times * freqs
    turns = turns - jnp.round(turns * (1.0 / SAMPLES)) * float(SAMPLES)
    half = turns * (math.pi / SAMPLES)
    square = half * half
    sine = jnp.full_like(half, -1.0 / math.factorial(11))
    for n in (9, 7, 5, 3, 1):
        sine = sine * square + (-1.0) ** (n // 2) / math.factorial(n)
    sine = sine * half
    cosine = jnp.full_like(half, 1.0 / math.factorial(12))
    for n in (10, 8, 6, 4, 2, 0):
        cosine = cosine * square + (-1.0) ** (n // 2) / math.factorial(n)
    return 1.0 - 2.0 * sine * sine, -2.0 * sine * cosine


def spectra_kernel(
    dims, first_ref, records_ref, out_ref, rec, basis, twiddle, acc, part_out, part_in, white,
    load_sem, rep_sems, z_send, z_recv, x_send, x_recv, own_send, own_recv, fwd_send, fwd_recv,
):
    bands, wins, band_bins, groups, blocks, chunks = dims
    total_groups = bands * groups
    band = lax.axis_index("band")
    win = lax.axis_index("win")
    rep = lax.axis_index("rep")
    other = 1 - rep

    def load(block):
        rows = pl.ds(pl.multiple_of(block * ROWS, ROWS), ROWS)
        return pltpu.make_async_copy(
            records_ref.at[:, rows, :], rec.at[:, rows, :], load_sem.at[block]
        )

    for block in reversed(range(blocks)):
        load(block).start()

    barrier = pltpu.get_barrier_semaphore()
    pl.semaphore_signal(barrier, inc=1, device_id={"rep": other}, device_id_type=MESH)
    for step in range(1, bands):
        pl.semaphore_signal(
            barrier, inc=1, device_id={"band": (band + step) % bands}, device_id_type=MESH
        )
    for step in range(1, wins):
        pl.semaphore_signal(
            barrier, inc=1, device_id={"win": (win + step) % wins}, device_id_type=MESH
        )

    base = (rep * (blocks * ROWS)).astype(jnp.float32)
    lane = lax.broadcasted_iota(jnp.int32, (SUB, LANES), 1).astype(jnp.float32)
    row = lax.broadcasted_iota(jnp.int32, (SUB, LANES), 0)
    first = first_ref[0]

    def build(group, _):
        local = (group % groups) * SUB + row
        freqs = (first + (group // groups) * band_bins + local).astype(jnp.float32)
        real, imag = rotor(base + lane, freqs)
        if band_bins % SUB:
            real = jnp.where(local < band_bins, real, 0.0)
            imag = jnp.where(local < band_bins, imag, 0.0)
        turn_real, turn_imag = rotor(float(LANES), freqs)
        block_real, block_imag = rotor(float(ROWS), freqs)
        twiddle[0, group] = block_real
        twiddle[1, group] = block_imag
        rows = pl.ds(pl.multiple_of(group * 2 * SUB, 2 * SUB), 2 * SUB)
        for part in range(ROWS // LANES):
            basis[rows, part * LANES : (part + 1) * LANES] = jnp.concatenate(
                [real, imag], axis=0
            ).astype(jnp.bfloat16)
            real, imag = (
                real * turn_real - imag * turn_imag,
                real * turn_imag + imag * turn_real,
            )
        return 0

    lax.fori_loop(0, total_groups, build, 0, unroll=2)
    acc[...] = jnp.zeros_like(acc)
    span = total_groups // chunks

    def transform(index, _):
        block = blocks - 1 - index
        load(block).wait()
        rows = pl.ds(pl.multiple_of(block * ROWS, ROWS), ROWS)
        both = jnp.concatenate([rec[0, rows, :], rec[1, rows, :]], axis=1)
        for chunk in range(chunks):
            product = jnp.dot(
                basis[chunk * span * 2 * SUB : (chunk + 1) * span * 2 * SUB, :],
                both,
                preferred_element_type=jnp.float32,
            ).reshape(span, 2, SUB, 2 * LANES)
            here = slice(chunk * span, (chunk + 1) * span)
            turn_real = twiddle[0, here]
            turn_imag = twiddle[1, here]
            for window in range(2):
                lanes = slice(window * LANES, (window + 1) * LANES)
                real = acc[window, here, 0]
                imag = acc[window, here, 1]
                acc[window, here, 0] = product[:, 0, :, lanes] + (
                    real * turn_real - imag * turn_imag
                )
                acc[window, here, 1] = product[:, 1, :, lanes] + (
                    real * turn_imag + imag * turn_real
                )
        return 0

    lax.fori_loop(0, blocks, transform, 0)
    part_out[...] = acc[other].reshape(part_out.shape).astype(jnp.bfloat16)
    pl.semaphore_wait(barrier, 1 + (bands - 1) + (wins - 1))
    exchange = pltpu.make_async_remote_copy(
        src_ref=part_out, dst_ref=part_in, send_sem=rep_sems.at[0], recv_sem=rep_sems.at[1],
        device_id={"rep": other}, device_id_type=MESH,
    )
    exchange.start()
    exchange.wait()

    spectrum = acc[rep] + part_in[...].astype(jnp.float32).reshape(total_groups, 2, SUB, LANES)
    acc[rep] = spectrum
    power = jnp.sum(jnp.sum(spectrum * spectrum, axis=1), axis=0)
    level = jnp.sqrt(jnp.sum(power, axis=0, keepdims=True) * (1.0 / NBINS) + 1e-06)
    floor = jnp.broadcast_to(water_level * level, (SUB, LANES))

    def whiten(group, _):
        pair = acc[rep, group]
        real, imag = pair[0], pair[1]
        scale = 1.0 / (jnp.sqrt(real * real + imag * imag) + floor)
        rows = pl.ds(pl.multiple_of((group % groups) * 2 * SUB, 2 * SUB), 2 * SUB)
        white[group // groups, rows, :] = jnp.concatenate(
            [real * scale, imag * scale], axis=0
        ).astype(jnp.bfloat16)
        return 0

    lax.fori_loop(0, total_groups, whiten, 0, unroll=4)

    mine = win * 2 + rep

    def to_band(step):
        target = (band + step) % bands
        return pltpu.make_async_remote_copy(
            src_ref=white.at[target], dst_ref=out_ref.at[mine, band],
            send_sem=z_send.at[step], recv_sem=z_recv.at[step],
            device_id={"band": target}, device_id_type=MESH,
        )

    def to_win(step, hop, source):
        return pltpu.make_async_remote_copy(
            src_ref=out_ref.at[mine, source], dst_ref=out_ref.at[mine, source],
            send_sem=x_send.at[hop, step], recv_sem=x_recv.at[hop, step],
            device_id={"win": (win + hop) % wins}, device_id_type=MESH,
        )

    def to_rep(step, source):
        return pltpu.make_async_remote_copy(
            src_ref=out_ref.at[mine, source], dst_ref=out_ref.at[mine, source],
            send_sem=own_send.at[step], recv_sem=own_recv.at[step],
            device_id={"rep": other}, device_id_type=MESH,
        )

    def forward(step, hop, source):
        window = ((win - hop + wins) % wins) * 2 + rep
        return pltpu.make_async_remote_copy(
            src_ref=out_ref.at[window, source], dst_ref=out_ref.at[window, source],
            send_sem=fwd_send.at[hop, step], recv_sem=fwd_recv.at[hop, step],
            device_id={"rep": other}, device_id_type=MESH,
        )

    for step in range(1, bands):
        to_band(step).start()
    out_ref[mine, band] = white[band]
    for step in range(bands):
        source = (band - step + bands) % bands
        if step:
            to_band(step).wait_recv()
        for hop in range(1, wins):
            to_win(step, hop, source).start()
        to_rep(step, source).start()
        if step:
            last = (band - step + 1 + bands) % bands
            for hop in range(1, wins):
                to_win(step - 1, hop, last).wait_recv()
                forward(step - 1, hop, last).start()
    last = (band + 1) % bands
    for hop in range(1, wins):
        to_win(bands - 1, hop, last).wait_recv()
        forward(bands - 1, hop, last).start()
    for step in range(bands):
        source = (band - step + bands) % bands
        if step:
            to_band(step).wait_send()
        to_rep(step, source).wait()
        for hop in range(1, wins):
            to_win(step, hop, source).wait_send()
            forward(step, hop, source).wait()


def cross_kernel(windows, share, slots, pairs_ref, counts_ref, white_ref, out_ref):
    rep = lax.axis_index("rep")
    shift = lax.axis_index("win") * share
    group = pl.program_id(0)
    rows = pl.ds(pl.multiple_of(group * 2 * SUB, 2 * SUB), 2 * SUB)
    depth = windows * 2 * SUB
    bins = lax.broadcasted_iota(jnp.int32, (share, depth), 1) % SUB
    for slot in range(slots):
        place = rep * slots + slot
        scale = jnp.where(place < counts_ref[0], 1.0 / windows, 0.0).astype(jnp.float32)
        left = white_ref[:, pairs_ref[0, place, 0], rows, :].reshape(depth, BLOCK)
        left = left.astype(jnp.float32) * scale
        left = pltpu.roll(left, (BLOCK - shift) % BLOCK, 1)
        left = left.T[:share, :]
        spread = jnp.concatenate(
            [jnp.where(bins == index, left, 0.0) for index in range(SUB)], axis=0
        ).astype(jnp.bfloat16)
        right = white_ref[:, pairs_ref[0, place, 1], rows, :].astype(jnp.float32)
        turned = jnp.concatenate([-right[:, SUB:], right[:, :SUB]], axis=1)
        both = jnp.concatenate(
            [right.reshape(depth, BLOCK), turned.reshape(depth, BLOCK)], axis=1
        ).astype(jnp.bfloat16)
        out_ref[:, slot] = jnp.dot(spread, both, preferred_element_type=jnp.float32).reshape(
            SUB, share, 2 * BLOCK
        )


def shards(bands, wins, records, bin_first, pair_blocks, pair_counts):
    _, half_rows, _ = records.shape
    band_bins = NBINS // bands
    groups = -(-band_bins // SUB)
    blocks = half_rows // ROWS
    total_groups = bands * groups
    chunks = 2
    windows = wins * 2
    doubled = groups * 2 * SUB
    slots = pair_blocks.shape[1] // 2
    share = BLOCK // wins
    dma = pltpu.SemaphoreType.DMA
    everything = pl.pallas_call(
        functools.partial(spectra_kernel, (bands, wins, band_bins, groups, blocks, chunks)),
        out_shape=jax.ShapeDtypeStruct((windows, bands, doubled, LANES), jnp.bfloat16),
        in_specs=[pl.BlockSpec(memory_space=pltpu.SMEM), pl.BlockSpec(memory_space=pl.ANY)],
        out_specs=pl.BlockSpec(memory_space=pltpu.VMEM),
        scratch_shapes=[
            pltpu.VMEM((2, half_rows, LANES), jnp.bfloat16),
            pltpu.VMEM((total_groups * 2 * SUB, ROWS), jnp.bfloat16),
            pltpu.VMEM((2, total_groups, SUB, LANES), jnp.float32),
            pltpu.VMEM((2, total_groups, 2, SUB, LANES), jnp.float32),
            pltpu.VMEM((total_groups * 2 * SUB, LANES), jnp.bfloat16),
            pltpu.VMEM((total_groups * 2 * SUB, LANES), jnp.bfloat16),
            pltpu.VMEM((bands, doubled, LANES), jnp.bfloat16),
            dma((blocks,)),
            dma((2,)),
            dma((bands,)),
            dma((bands,)),
            dma((wins, bands)),
            dma((wins, bands)),
            dma((bands,)),
            dma((bands,)),
            dma((wins, bands)),
            dma((wins, bands)),
        ],
        compiler_params=pltpu.CompilerParams(
            collective_id=0, has_side_effects=True, vmem_limit_bytes=40 * 2**20
        ),
        name="spectra",
    )(bin_first, records)
    return pl.pallas_call(
        functools.partial(cross_kernel, windows, share, slots),
        out_shape=jax.ShapeDtypeStruct((band_bins, slots, share, 2 * BLOCK), jnp.float32),
        grid_spec=pltpu.PrefetchScalarGridSpec(
            num_scalar_prefetch=2,
            grid=(groups,),
            in_specs=[pl.BlockSpec(memory_space=pltpu.VMEM)],
            out_specs=pl.BlockSpec((SUB, slots, share, 2 * BLOCK), lambda g, *_: (g, 0, 0, 0)),
        ),
        compiler_params=pltpu.CompilerParams(vmem_limit_bytes=40 * 2**20),
        name="cross",
    )(pair_blocks, pair_counts, everything)


def solution(mesh):
    return jax.shard_map(
        functools.partial(shards, mesh.shape["band"], mesh.shape["win"]),
        mesh=mesh,
        in_specs=(P(("parts", "win"), "rep", "band"), P(), P("band", None, None), P("band")),
        out_specs=P(("parts", "band"), "rep", "win", None),
        check_vma=False,
    )
```

```python
import functools
import math

import jax
import jax.numpy as jnp
from jax import lax
from jax.experimental import pallas as pl
from jax.experimental.pallas import tpu as pltpu
from jax.sharding import PartitionSpec as P

SAMPLES = 15360
NBINS = 544
BLOCK = 128
LANES = 128
SUB = 8
ROWS = 1280
WIDE = 4
PIECES = 3
PER = 3
MESH = pl.DeviceIdType.MESH

water_level = 0.1


def rotor(times, freqs):
    turns = times * freqs
    turns = turns - jnp.round(turns * (1.0 / SAMPLES)) * float(SAMPLES)
    half = turns * (math.pi / SAMPLES)
    square = half * half
    sine = jnp.full_like(half, -1.0 / math.factorial(11))
    for n in (9, 7, 5, 3, 1):
        sine = sine * square + (-1.0) ** (n // 2) / math.factorial(n)
    sine = sine * half
    cosine = jnp.full_like(half, 1.0 / math.factorial(12))
    for n in (10, 8, 6, 4, 2, 0):
        cosine = cosine * square + (-1.0) ** (n // 2) / math.factorial(n)
    return 1.0 - 2.0 * sine * sine, -2.0 * sine * cosine


def spectra_kernel(
    dims, first_ref, records_ref, out_ref, rec, basis, twiddle, acc, part_out, part_in, white,
    load_sem, rep_sems, z_send, z_recv, x_send, x_recv, own_send, own_recv, fwd_send, fwd_recv,
):
    bands, wins, band_bins, groups, blocks, chunks = dims
    total_groups = bands * groups
    band = lax.axis_index("band")
    win = lax.axis_index("win")
    rep = lax.axis_index("rep")
    other = 1 - rep

    def load(block):
        rows = pl.ds(pl.multiple_of(block * ROWS, ROWS), ROWS)
        return pltpu.make_async_copy(
            records_ref.at[:, rows, :], rec.at[:, rows, :], load_sem.at[block]
        )

    for block in reversed(range(blocks)):
        load(block).start()

    barrier = pltpu.get_barrier_semaphore()
    pl.semaphore_signal(barrier, inc=1, device_id={"rep": other}, device_id_type=MESH)
    for step in range(1, bands):
        pl.semaphore_signal(
            barrier, inc=1, device_id={"band": (band + step) % bands}, device_id_type=MESH
        )
    for step in range(1, wins):
        pl.semaphore_signal(
            barrier, inc=1, device_id={"win": (win + step) % wins}, device_id_type=MESH
        )

    base = (rep * (blocks * ROWS)).astype(jnp.float32)
    lane = lax.broadcasted_iota(jnp.int32, (WIDE, SUB, LANES), 2).astype(jnp.float32)
    row = lax.broadcasted_iota(jnp.int32, (WIDE, SUB, LANES), 1)
    first = first_ref[0]

    def build(index, _):
        ids = index * WIDE + lax.broadcasted_iota(jnp.int32, (WIDE, SUB, LANES), 0)
        local = (ids % groups) * SUB + row
        freqs = (first + (ids // groups) * band_bins + local).astype(jnp.float32)
        real, imag = rotor(base + lane, freqs)
        if band_bins % SUB:
            real = jnp.where(local < band_bins, real, 0.0)
            imag = jnp.where(local < band_bins, imag, 0.0)
        turn_real, turn_imag = rotor(float(LANES), freqs)
        block_real, block_imag = rotor(float(ROWS), freqs)
        here = pl.ds(index * WIDE, WIDE)
        twiddle[0, here] = block_real
        twiddle[1, here] = block_imag
        rows = pl.ds(pl.multiple_of(index * (WIDE * 2 * SUB), WIDE * 2 * SUB), WIDE * 2 * SUB)
        for part in range(ROWS // LANES):
            basis[rows, part * LANES : (part + 1) * LANES] = (
                jnp.concatenate([real, imag], axis=1)
                .reshape(WIDE * 2 * SUB, LANES)
                .astype(jnp.bfloat16)
            )
            real, imag = (
                real * turn_real - imag * turn_imag,
                real * turn_imag + imag * turn_real,
            )
        return 0

    lax.fori_loop(0, total_groups // WIDE, build, 0)
    acc[...] = jnp.zeros_like(acc)
    span = total_groups // chunks

    def transform(index, _):
        block = blocks - 1 - index
        load(block).wait()
        rows = pl.ds(pl.multiple_of(block * ROWS, ROWS), ROWS)
        both = jnp.concatenate([rec[0, rows, :], rec[1, rows, :]], axis=1)
        for chunk in range(chunks):
            product = jnp.dot(
                basis[chunk * span * 2 * SUB : (chunk + 1) * span * 2 * SUB, :],
                both,
                preferred_element_type=jnp.float32,
            ).reshape(span, 2, SUB, 2 * LANES)
            here = slice(chunk * span, (chunk + 1) * span)
            turn_real = twiddle[0, here]
            turn_imag = twiddle[1, here]
            for window in range(2):
                lanes = slice(window * LANES, (window + 1) * LANES)
                real = acc[window, here, 0]
                imag = acc[window, here, 1]
                acc[window, here, 0] = product[:, 0, :, lanes] + (
                    real * turn_real - imag * turn_imag
                )
                acc[window, here, 1] = product[:, 1, :, lanes] + (
                    real * turn_imag + imag * turn_real
                )
        return 0

    lax.fori_loop(0, blocks, transform, 0)
    part_out[...] = acc[other].reshape(part_out.shape).astype(jnp.bfloat16)
    pl.semaphore_wait(barrier, 1 + (bands - 1) + (wins - 1))
    exchange = pltpu.make_async_remote_copy(
        src_ref=part_out, dst_ref=part_in, send_sem=rep_sems.at[0], recv_sem=rep_sems.at[1],
        device_id={"rep": other}, device_id_type=MESH,
    )
    exchange.start()
    exchange.wait()

    spectrum = acc[rep] + part_in[...].astype(jnp.float32).reshape(total_groups, 2, SUB, LANES)
    acc[rep] = spectrum
    power = jnp.sum(jnp.sum(spectrum * spectrum, axis=1), axis=0)
    level = jnp.sqrt(jnp.sum(power, axis=0, keepdims=True) * (1.0 / NBINS) + 1e-06)
    floor = jnp.broadcast_to(water_level * level, (SUB, LANES))

    def whiten(group, _):
        pair = acc[rep, group]
        real, imag = pair[0], pair[1]
        scale = 1.0 / (jnp.sqrt(real * real + imag * imag) + floor)
        rows = pl.ds(pl.multiple_of((group % groups) * 2 * SUB, 2 * SUB), 2 * SUB)
        white[group // groups, rows, :] = jnp.concatenate(
            [real * scale, imag * scale], axis=0
        ).astype(jnp.bfloat16)
        return 0

    lax.fori_loop(0, total_groups, whiten, 0, unroll=4)

    mine = win * 2 + rep

    cuts = [2 * SUB * (groups * piece // PIECES) for piece in range(PIECES + 1)]

    def span_of(piece):
        return pl.ds(cuts[piece], cuts[piece + 1] - cuts[piece])

    def source(step):
        return (band - step + bands) % bands

    def to_band(step, piece):
        target = (band + step) % bands
        return pltpu.make_async_remote_copy(
            src_ref=white.at[target, span_of(piece)],
            dst_ref=out_ref.at[mine, band, span_of(piece)],
            send_sem=z_send.at[step, piece], recv_sem=z_recv.at[step, piece],
            device_id={"band": target}, device_id_type=MESH,
        )

    def to_win(step, piece, hop):
        block = out_ref.at[mine, source(step), span_of(piece)]
        return pltpu.make_async_remote_copy(
            src_ref=block, dst_ref=block,
            send_sem=x_send.at[hop, step, piece], recv_sem=x_recv.at[hop, step, piece],
            device_id={"win": (win + hop) % wins}, device_id_type=MESH,
        )

    def to_rep(step, piece):
        block = out_ref.at[mine, source(step), span_of(piece)]
        return pltpu.make_async_remote_copy(
            src_ref=block, dst_ref=block,
            send_sem=own_send.at[step, piece], recv_sem=own_recv.at[step, piece],
            device_id={"rep": other}, device_id_type=MESH,
        )

    def forward(step, piece, hop):
        window = ((win - hop + wins) % wins) * 2 + rep
        block = out_ref.at[window, source(step), span_of(piece)]
        return pltpu.make_async_remote_copy(
            src_ref=block, dst_ref=block,
            send_sem=fwd_send.at[hop, step, piece], recv_sem=fwd_recv.at[hop, step, piece],
            device_id={"rep": other}, device_id_type=MESH,
        )

    def relay(item):
        step, piece = item
        for hop in range(1, wins):
            to_win(step, piece, hop).wait_recv()
            forward(step, piece, hop).start()

    for piece in range(PIECES):
        for step in range(1, bands):
            to_band(step, piece).start()
    out_ref[mine, band, : cuts[-1]] = white[band]
    items = [(0, piece) for piece in range(PIECES)]
    items += [(step, piece) for piece in range(PIECES) for step in range(1, bands)]
    for place, (step, piece) in enumerate(items):
        if step:
            to_band(step, piece).wait_recv()
        for hop in range(1, wins):
            to_win(step, piece, hop).start()
        to_rep(step, piece).start()
        if place >= PIECES:
            relay(items[place - PIECES])
    for item in items[-PIECES:]:
        relay(item)
    for step, piece in items:
        if step:
            to_band(step, piece).wait_send()
        to_rep(step, piece).wait()
        for hop in range(1, wins):
            to_win(step, piece, hop).wait_send()
            forward(step, piece, hop).wait()


def cross_kernel(windows, share, slots, per, pairs_ref, counts_ref, white_ref, out_ref):
    rep = lax.axis_index("rep")
    shift = lax.axis_index("win") * share
    depth = windows * 2 * SUB
    bins = lax.broadcasted_iota(jnp.int32, (share, depth), 1) % SUB
    masks = [jnp.where(bins == index, 1.0, 0.0).astype(jnp.bfloat16) for index in range(SUB)]
    for part in range(per):
        start = (pl.program_id(0) * per + part) * 2 * SUB
        rows = pl.ds(pl.multiple_of(start, 2 * SUB), 2 * SUB)
        for slot in range(slots):
            place = rep * slots + slot
            scale = jnp.where(place < counts_ref[0], 1.0 / windows, 0.0).astype(jnp.float32)
            left = white_ref[:, pairs_ref[0, 0, place], rows, :].reshape(depth, BLOCK)
            left = left.astype(jnp.float32) * scale
            left = pltpu.roll(left, (BLOCK - shift) % BLOCK, 1)
            left = left.T[:share, :].astype(jnp.bfloat16)
            spread = jnp.concatenate([left * mask for mask in masks], axis=0)
            right = white_ref[:, pairs_ref[0, 1, place], rows, :].astype(jnp.float32)
            turned = jnp.concatenate([-right[:, SUB:], right[:, :SUB]], axis=1)
            both = jnp.concatenate(
                [right.reshape(depth, BLOCK), turned.reshape(depth, BLOCK)], axis=1
            ).astype(jnp.bfloat16)
            out_ref[part * SUB : (part + 1) * SUB, slot] = jnp.dot(
                spread, both, preferred_element_type=jnp.float32
            ).reshape(SUB, share, 2 * BLOCK)


def shards(bands, wins, records, bin_first, pair_blocks, pair_counts):
    _, half_rows, _ = records.shape
    band_bins = NBINS // bands
    groups = -(-band_bins // SUB)
    blocks = half_rows // ROWS
    total_groups = bands * groups
    chunks = 2
    windows = wins * 2
    doubled = groups * 2 * SUB
    slots = pair_blocks.shape[1] // 2
    share = BLOCK // wins
    dma = pltpu.SemaphoreType.DMA
    everything = pl.pallas_call(
        functools.partial(spectra_kernel, (bands, wins, band_bins, groups, blocks, chunks)),
        out_shape=jax.ShapeDtypeStruct((windows, bands, -(-groups // PER) * PER * 2 * SUB, LANES), jnp.bfloat16),
        in_specs=[pl.BlockSpec(memory_space=pltpu.SMEM), pl.BlockSpec(memory_space=pl.ANY)],
        out_specs=pl.BlockSpec(memory_space=pltpu.VMEM),
        scratch_shapes=[
            pltpu.VMEM((2, half_rows, LANES), jnp.bfloat16),
            pltpu.VMEM((total_groups * 2 * SUB, ROWS), jnp.bfloat16),
            pltpu.VMEM((2, total_groups, SUB, LANES), jnp.float32),
            pltpu.VMEM((2, total_groups, 2, SUB, LANES), jnp.float32),
            pltpu.VMEM((total_groups * 2 * SUB, LANES), jnp.bfloat16),
            pltpu.VMEM((total_groups * 2 * SUB, LANES), jnp.bfloat16),
            pltpu.VMEM((bands, doubled, LANES), jnp.bfloat16),
            dma((blocks,)),
            dma((2,)),
            dma((bands, PIECES)),
            dma((bands, PIECES)),
            dma((wins, bands, PIECES)),
            dma((wins, bands, PIECES)),
            dma((bands, PIECES)),
            dma((bands, PIECES)),
            dma((wins, bands, PIECES)),
            dma((wins, bands, PIECES)),
        ],
        compiler_params=pltpu.CompilerParams(
            collective_id=0, has_side_effects=True, vmem_limit_bytes=605 * 2**20 // 10
        ),
        name="spectra",
    )(bin_first, records)
    return pl.pallas_call(
        functools.partial(cross_kernel, windows, share, slots, PER),
        out_shape=jax.ShapeDtypeStruct((band_bins, slots, share, 2 * BLOCK), jnp.float32),
        grid_spec=pltpu.PrefetchScalarGridSpec(
            num_scalar_prefetch=2,
            grid=(-(-groups // PER),),
            in_specs=[pl.BlockSpec(memory_space=pltpu.VMEM)],
            out_specs=pl.BlockSpec((PER * SUB, slots, share, 2 * BLOCK), lambda g, *_: (g, 0, 0, 0)),
        ),
        compiler_params=pltpu.CompilerParams(vmem_limit_bytes=40 * 2**20),
        name="cross",
    )(jnp.swapaxes(pair_blocks, 1, 2), pair_counts, everything)


def solution(mesh):
    return jax.shard_map(
        functools.partial(shards, mesh.shape["band"], mesh.shape["win"]),
        mesh=mesh,
        in_specs=(P(("parts", "win"), "rep", "band"), P(), P("band", None, None), P("band")),
        out_specs=P(("parts", "band"), "rep", "win", None),
        check_vma=False,
    )
```

```python
import functools
import math

import jax
import jax.numpy as jnp
from jax import lax
from jax.experimental import pallas as pl
from jax.experimental.pallas import tpu as pltpu
from jax.sharding import PartitionSpec as P

SAMPLES = 15360
NBINS = 544
BLOCK = 128
LANES = 128
SUB = 8
ROWS = 1280
WIDE = 4
PIECES = 1
AHEAD = 1
LAG = 3
PER = 3
MESH = pl.DeviceIdType.MESH

water_level = 0.1


def rotor(times, freqs):
    turns = times * freqs
    turns = turns - jnp.round(turns * (1.0 / SAMPLES)) * float(SAMPLES)
    half = turns * (math.pi / SAMPLES)
    square = half * half
    sine = jnp.full_like(half, -1.0 / math.factorial(11))
    for n in (9, 7, 5, 3, 1):
        sine = sine * square + (-1.0) ** (n // 2) / math.factorial(n)
    sine = sine * half
    cosine = jnp.full_like(half, 1.0 / math.factorial(12))
    for n in (10, 8, 6, 4, 2, 0):
        cosine = cosine * square + (-1.0) ** (n // 2) / math.factorial(n)
    return 1.0 - 2.0 * sine * sine, -2.0 * sine * cosine


def spectra_kernel(
    dims, first_ref, records_ref, out_ref, rec, basis, twiddle, acc, part_out, part_in, white,
    load_sem, rep_sems, z_send, z_recv, x_send, x_recv, own_send, own_recv, fwd_send, fwd_recv,
):
    bands, wins, band_bins, groups, blocks, chunks = dims
    total_groups = bands * groups
    band = lax.axis_index("band")
    win = lax.axis_index("win")
    rep = lax.axis_index("rep")
    other = 1 - rep

    def load(block):
        rows = pl.ds(pl.multiple_of(block * ROWS, ROWS), ROWS)
        return pltpu.make_async_copy(
            records_ref.at[:, rows, :], rec.at[:, rows, :], load_sem.at[block]
        )

    for block in reversed(range(blocks)):
        load(block).start()

    barrier = pltpu.get_barrier_semaphore()
    pl.semaphore_signal(barrier, inc=1, device_id={"rep": other}, device_id_type=MESH)
    for step in range(1, bands):
        pl.semaphore_signal(
            barrier, inc=1, device_id={"band": (band + step) % bands}, device_id_type=MESH
        )
    for step in range(1, wins):
        pl.semaphore_signal(
            barrier, inc=1, device_id={"win": (win + step) % wins}, device_id_type=MESH
        )

    base = (rep * (blocks * ROWS)).astype(jnp.float32)
    lane = lax.broadcasted_iota(jnp.int32, (WIDE, SUB, LANES), 2).astype(jnp.float32)
    row = lax.broadcasted_iota(jnp.int32, (WIDE, SUB, LANES), 1)
    first = first_ref[0]

    def build(index, _):
        ids = index * WIDE + lax.broadcasted_iota(jnp.int32, (WIDE, SUB, LANES), 0)
        local = (ids % groups) * SUB + row
        freqs = (first + (ids // groups) * band_bins + local).astype(jnp.float32)
        real, imag = rotor(base + lane, freqs)
        if band_bins % SUB:
            real = jnp.where(local < band_bins, real, 0.0)
            imag = jnp.where(local < band_bins, imag, 0.0)
        turn_real, turn_imag = rotor(float(LANES), freqs)
        block_real, block_imag = rotor(float(ROWS), freqs)
        here = pl.ds(index * WIDE, WIDE)
        twiddle[0, here] = block_real
        twiddle[1, here] = block_imag
        rows = pl.ds(pl.multiple_of(index * (WIDE * 2 * SUB), WIDE * 2 * SUB), WIDE * 2 * SUB)
        for part in range(ROWS // LANES):
            basis[rows, part * LANES : (part + 1) * LANES] = (
                jnp.concatenate([real, imag], axis=1)
                .reshape(WIDE * 2 * SUB, LANES)
                .astype(jnp.bfloat16)
            )
            real, imag = (
                real * turn_real - imag * turn_imag,
                real * turn_imag + imag * turn_real,
            )
        return 0

    lax.fori_loop(0, total_groups // WIDE, build, 0)
    acc[...] = jnp.zeros_like(acc)
    span = total_groups // chunks

    def transform(index, _):
        block = blocks - 1 - index
        load(block).wait()
        rows = pl.ds(pl.multiple_of(block * ROWS, ROWS), ROWS)
        both = jnp.concatenate([rec[0, rows, :], rec[1, rows, :]], axis=1)
        for chunk in range(chunks):
            product = jnp.dot(
                basis[chunk * span * 2 * SUB : (chunk + 1) * span * 2 * SUB, :],
                both,
                preferred_element_type=jnp.float32,
            ).reshape(span, 2, SUB, 2 * LANES)
            here = slice(chunk * span, (chunk + 1) * span)
            turn_real = twiddle[0, here]
            turn_imag = twiddle[1, here]
            for window in range(2):
                lanes = slice(window * LANES, (window + 1) * LANES)
                real = acc[window, here, 0]
                imag = acc[window, here, 1]
                acc[window, here, 0] = product[:, 0, :, lanes] + (
                    real * turn_real - imag * turn_imag
                )
                acc[window, here, 1] = product[:, 1, :, lanes] + (
                    real * turn_imag + imag * turn_real
                )
        return 0

    lax.fori_loop(0, blocks, transform, 0)
    part_out[...] = acc[other].reshape(part_out.shape).astype(jnp.bfloat16)
    pl.semaphore_wait(barrier, 1 + (bands - 1) + (wins - 1))
    exchange = pltpu.make_async_remote_copy(
        src_ref=part_out, dst_ref=part_in, send_sem=rep_sems.at[0], recv_sem=rep_sems.at[1],
        device_id={"rep": other}, device_id_type=MESH,
    )
    exchange.start()
    exchange.wait()

    spectrum = acc[rep] + part_in[...].astype(jnp.float32).reshape(total_groups, 2, SUB, LANES)
    acc[rep] = spectrum
    power = jnp.sum(jnp.sum(spectrum * spectrum, axis=1), axis=0)
    level = jnp.sqrt(jnp.sum(power, axis=0, keepdims=True) * (1.0 / NBINS) + 1e-06)
    floor = jnp.broadcast_to(water_level * level, (SUB, LANES))

    def whiten(group, _):
        pair = acc[rep, group]
        real, imag = pair[0], pair[1]
        scale = 1.0 / (jnp.sqrt(real * real + imag * imag) + floor)
        rows = pl.ds(pl.multiple_of((group % groups) * 2 * SUB, 2 * SUB), 2 * SUB)
        white[group // groups, rows, :] = jnp.concatenate(
            [real * scale, imag * scale], axis=0
        ).astype(jnp.bfloat16)
        return 0

    lax.fori_loop(0, total_groups, whiten, 0, unroll=4)

    mine = win * 2 + rep

    cuts = [2 * SUB * (groups * piece // PIECES) for piece in range(PIECES + 1)]

    def span_of(piece):
        return pl.ds(cuts[piece], cuts[piece + 1] - cuts[piece])

    def source(step):
        return (band - step + bands) % bands

    def to_band(step, piece):
        target = (band + step) % bands
        return pltpu.make_async_remote_copy(
            src_ref=white.at[target, span_of(piece)],
            dst_ref=out_ref.at[mine, band, span_of(piece)],
            send_sem=z_send.at[step, piece], recv_sem=z_recv.at[step, piece],
            device_id={"band": target}, device_id_type=MESH,
        )

    def to_win(step, piece, hop):
        block = out_ref.at[mine, source(step), span_of(piece)]
        return pltpu.make_async_remote_copy(
            src_ref=block, dst_ref=block,
            send_sem=x_send.at[hop, step, piece], recv_sem=x_recv.at[hop, step, piece],
            device_id={"win": (win + hop) % wins}, device_id_type=MESH,
        )

    def to_rep(step, piece):
        block = out_ref.at[mine, source(step), span_of(piece)]
        return pltpu.make_async_remote_copy(
            src_ref=block, dst_ref=block,
            send_sem=own_send.at[step, piece], recv_sem=own_recv.at[step, piece],
            device_id={"rep": other}, device_id_type=MESH,
        )

    def forward(step, piece, hop):
        window = ((win - hop + wins) % wins) * 2 + rep
        block = out_ref.at[window, source(step), span_of(piece)]
        return pltpu.make_async_remote_copy(
            src_ref=block, dst_ref=block,
            send_sem=fwd_send.at[hop, step, piece], recv_sem=fwd_recv.at[hop, step, piece],
            device_id={"rep": other}, device_id_type=MESH,
        )

    def relay(item):
        step, piece = item
        for hop in range(1, wins):
            to_win(step, piece, hop).wait_recv()
            forward(step, piece, hop).start()

    for piece in range(min(AHEAD, PIECES)):
        for step in range(1, bands):
            to_band(step, piece).start()
    out_ref[mine, band, : cuts[-1]] = white[band]
    items = [(0, piece) for piece in range(PIECES)]
    items += [(step, piece) for piece in range(PIECES) for step in range(1, bands)]
    for place, (step, piece) in enumerate(items):
        if step:
            to_band(step, piece).wait_recv()
        for hop in range(1, wins):
            to_win(step, piece, hop).start()
        to_rep(step, piece).start()
        if step == bands - 1 and piece + AHEAD < PIECES:
            for later in range(1, bands):
                to_band(later, piece + AHEAD).start()
        if place >= LAG:
            relay(items[place - LAG])
    for item in items[-LAG:]:
        relay(item)
    for step, piece in items:
        if step:
            to_band(step, piece).wait_send()
        to_rep(step, piece).wait()
        for hop in range(1, wins):
            to_win(step, piece, hop).wait_send()
            forward(step, piece, hop).wait()


def cross_kernel(windows, share, slots, per, pairs_ref, counts_ref, white_ref, out_ref):
    rep = lax.axis_index("rep")
    shift = lax.axis_index("win") * share
    depth = windows * 2 * SUB
    bins = lax.broadcasted_iota(jnp.int32, (share, depth), 1) % SUB
    masks = [jnp.where(bins == index, 1.0, 0.0).astype(jnp.bfloat16) for index in range(SUB)]
    for part in range(per):
        rows = slice(part * 2 * SUB, (part + 1) * 2 * SUB)
        for slot in range(slots):
            place = rep * slots + slot
            scale = jnp.where(place < counts_ref[0], 1.0 / windows, 0.0).astype(jnp.float32)
            left = white_ref[:, pairs_ref[0, 0, place], rows, :].reshape(depth, BLOCK)
            left = left.astype(jnp.float32) * scale
            left = pltpu.roll(left, (BLOCK - shift) % BLOCK, 1)
            left = left.T[:share, :].astype(jnp.bfloat16)
            spread = jnp.concatenate([left * mask for mask in masks], axis=0)
            right = white_ref[:, pairs_ref[0, 1, place], rows, :].astype(jnp.float32)
            turned = jnp.concatenate([-right[:, SUB:], right[:, :SUB]], axis=1)
            both = jnp.concatenate(
                [right.reshape(depth, BLOCK), turned.reshape(depth, BLOCK)], axis=1
            ).astype(jnp.bfloat16)
            out_ref[part * SUB : (part + 1) * SUB, slot] = jnp.dot(
                spread, both, preferred_element_type=jnp.float32
            ).reshape(SUB, share, 2 * BLOCK)


def shards(bands, wins, records, bin_first, pair_blocks, pair_counts):
    _, half_rows, _ = records.shape
    band_bins = NBINS // bands
    groups = -(-band_bins // SUB)
    blocks = half_rows // ROWS
    total_groups = bands * groups
    chunks = 2
    windows = wins * 2
    doubled = groups * 2 * SUB
    slots = pair_blocks.shape[1] // 2
    share = BLOCK // wins
    dma = pltpu.SemaphoreType.DMA
    everything = pl.pallas_call(
        functools.partial(spectra_kernel, (bands, wins, band_bins, groups, blocks, chunks)),
        out_shape=jax.ShapeDtypeStruct((windows, bands, -(-groups // PER) * PER * 2 * SUB, LANES), jnp.bfloat16),
        in_specs=[pl.BlockSpec(memory_space=pltpu.SMEM), pl.BlockSpec(memory_space=pl.ANY)],
        out_specs=pl.BlockSpec(memory_space=pltpu.VMEM),
        scratch_shapes=[
            pltpu.VMEM((2, half_rows, LANES), jnp.bfloat16),
            pltpu.VMEM((total_groups * 2 * SUB, ROWS), jnp.bfloat16),
            pltpu.VMEM((2, total_groups, SUB, LANES), jnp.float32),
            pltpu.VMEM((2, total_groups, 2, SUB, LANES), jnp.float32),
            pltpu.VMEM((total_groups * 2 * SUB, LANES), jnp.bfloat16),
            pltpu.VMEM((total_groups * 2 * SUB, LANES), jnp.bfloat16),
            pltpu.VMEM((bands, doubled, LANES), jnp.bfloat16),
            dma((blocks,)),
            dma((2,)),
            dma((bands, PIECES)),
            dma((bands, PIECES)),
            dma((wins, bands, PIECES)),
            dma((wins, bands, PIECES)),
            dma((bands, PIECES)),
            dma((bands, PIECES)),
            dma((wins, bands, PIECES)),
            dma((wins, bands, PIECES)),
        ],
        compiler_params=pltpu.CompilerParams(
            collective_id=0, has_side_effects=True, vmem_limit_bytes=605 * 2**20 // 10
        ),
        name="spectra",
    )(bin_first, records)
    return pl.pallas_call(
        functools.partial(cross_kernel, windows, share, slots, PER),
        out_shape=jax.ShapeDtypeStruct((band_bins, slots, share, 2 * BLOCK), jnp.float32),
        grid_spec=pltpu.PrefetchScalarGridSpec(
            num_scalar_prefetch=2,
            grid=(-(-groups // PER),),
            in_specs=[
                pl.BlockSpec((windows, bands, PER * 2 * SUB, LANES), lambda g, *_: (0, 0, g, 0))
            ],
            out_specs=pl.BlockSpec((PER * SUB, slots, share, 2 * BLOCK), lambda g, *_: (g, 0, 0, 0)),
        ),
        compiler_params=pltpu.CompilerParams(vmem_limit_bytes=605 * 2**20 // 10),
        name="cross",
    )(jnp.swapaxes(pair_blocks, 1, 2), pair_counts, everything)


def solution(mesh):
    return jax.shard_map(
        functools.partial(shards, mesh.shape["band"], mesh.shape["win"]),
        mesh=mesh,
        in_specs=(P(("parts", "win"), "rep", "band"), P(), P("band", None, None), P("band")),
        out_specs=P(("parts", "band"), "rep", "win", None),
        check_vma=False,
    )
```
